128 devices in a mesh: dp: 16 (over x, y), ctx: 8 (over z, core).
Axes of the slice: x: 4, y: 4, z: 4, core: 2. Of those that a mesh axis runs over, the one named last changes fastest.
Arguments:
- tokens: bfloat16 [16, 2048, 1024], P('dp', 'ctx'), may hold values from -6 to 6
- cotangent: bfloat16 [16, 2048, 1024], P('dp', 'ctx'), may hold values from -6 to 6
- proj_weight: bfloat16 [1024, 3072], replicated, may hold values from -0.1875 to 0.1875
- segment: int32 [16, 2048], P('dp', 'ctx'), may hold values from 0 to 2, never falling along the last dimension, each value on 1 to 1024 neighbouring positions
Outputs:
- output: bfloat16 [16, 2048, 1024], P('dp', 'ctx')
- grad_tokens: bfloat16 [16, 2048, 1024], P('dp', 'ctx')
- grad_weight: float32 [1024, 3072], replicated
The draws below stay inside these ranges and needn't reach their ends.
Inputs may be any that keep to these rules, and one draw needn't show every extreme that they name: `segment`: segment numbers never fall along a group's tokens; every history holds 1 to 1024 tokens and one of each group exactly 1024.
All inputs are finite; a program needn't handle non-finite values.
Results may differ from the reference program's by a relative error of at most 0.014.
Values may be sent and summed in bfloat16 or wider, within the bound.
No kernel may reach another device: no remote copies, remote signals or barrier semaphores. Data moves between devices by JAX's collectives and lax.ppermute only.
A program may use at most 128 MiB of HBM per device.

```python
import math
import jax
import jax.numpy as jnp
import numpy as np
from jax import lax

D = 1024
HEADS = 8
HEAD = 128
TOK_DEV = 256
SEQS = 3
GROUPS = 16
TOK_G = 2048
SEG_MOST = 1024
ALL_TOKENS = 32768
N_CTX = 8


def levels(key, extent, cuts, least, top_value):
    level = 1.0
    for dim, parts in cuts:
        heights = jax.random.uniform(jax.random.fold_in(jax.random.fold_in(key, 6), dim), (parts,), jnp.float32, least / len(cuts), top_value / len(cuts))
        level = level * jnp.repeat(jnp.exp(heights), extent[dim] // parts).reshape((-1,) + (1,) * (len(extent) - 1 - dim))
    return level


def length_profile(amount, total, limit, skew):
    loads = [(1 << 20) // math.isqrt(grade ** skew) + 1 for grade in range(2, amount + 1)]
    rest, holding = total - limit - (amount - 1), [1] * (amount - 1)
    while rest > 0:
        movable = [i for i in range(amount - 1) if holding[i] < limit]
        mass, remaining = sum([loads[i] for i in movable]), rest
        for i in movable:
            extra = min(limit - holding[i], max(1, remaining * loads[i] // mass), rest)
            holding[i] = holding[i] + extra
            rest = rest - extra
    return np.array([limit] + holding)


def ragged_sizes(own_key, count, total, reach, lean):
    if count == 2:
        one = jax.random.randint(own_key, (), max(1, total - reach), min(reach, total - 1) + 1)
        return jnp.stack([one, total - one])
    tallies = jnp.asarray(length_profile(count, total, reach, lean), jnp.int32)
    twos = (count - 1) // 2
    donor, sink = tallies[1:1 + 2 * twos:2], tallies[2:2 + 2 * twos:2]
    room = jnp.minimum(donor - 1, reach - sink)
    passed = jax.random.randint(jax.random.fold_in(own_key, 1), (twos,), 0, 1 << 20) % (room + 1)
    tallies = tallies.at[1:1 + 2 * twos:2].set(donor - passed).at[2:2 + 2 * twos:2].set(sink + passed)
    return tallies[jax.random.permutation(jax.random.fold_in(own_key, 2), count)]


def gaussian(stream_key, extent, width, most, split=(), kind=jnp.bfloat16):
    factor_of = levels(stream_key, extent, split, -0.22, 0.18) if split else 1.0
    result = jax.random.normal(stream_key, extent, jnp.float32) * width * factor_of
    return jnp.minimum(jnp.maximum(result, -most), most).astype(kind)


def setup_inputs(seed: int = 0) -> dict:
    key_list = jax.random.split(jax.random.key(seed), 5)
    return {
        "tokens": gaussian(key_list[0], (GROUPS, TOK_G, D), 1.0, 6.0, ((0, 16), (1, 8))),
        "cotangent": gaussian(key_list[1], (GROUPS, TOK_G, D), 1.0, 6.0, ((0, 16), (1, 8))),
        "proj_weight": gaussian(key_list[2], (D, 3 * D), D ** -0.5, 0.1875),
        "segment": jax.vmap(lambda own: jnp.searchsorted(jnp.cumsum(ragged_sizes(own, SEQS, TOK_G, SEG_MOST, 2)), jnp.arange(TOK_G), side="right"))(jax.random.split(key_list[3], GROUPS)).reshape((GROUPS, TOK_G)).astype(jnp.int32),
    }


EPS = 1e-05

def normalize(value):
    centred = value - lax.optimization_barrier(jnp.mean(value, axis=-1, keepdims=True))
    spread = lax.optimization_barrier(jnp.mean(centred * centred, axis=-1, keepdims=True))
    return centred * lax.rsqrt(spread + EPS)

def normalize_back(grad, value):
    centred = value - lax.optimization_barrier(jnp.mean(value, axis=-1, keepdims=True))
    factor = lax.rsqrt(lax.optimization_barrier(jnp.mean(centred * centred, axis=-1, keepdims=True)) + EPS)
    normal = centred * factor
    inner = grad - lax.optimization_barrier(jnp.mean(grad, axis=-1, keepdims=True))
    return factor * (inner - normal * lax.optimization_barrier(jnp.mean(grad * normal, axis=-1, keepdims=True)))

def silu_grad(value):
    sigma = jax.nn.sigmoid(value)
    return sigma * (1.0 + value * (1.0 - sigma))

def reference(tokens, cotangent, proj_weight, segment):
    scale = 1.0 / HEAD ** 0.5
    inv_most = 1.0 / SEG_MOST
    inv_root = 1.0 / ALL_TOKENS ** 0.5

    def one_group(total, items):
        x_tok, grad_out, seg_ids = items
        x_float = x_tok.astype(jnp.float32)
        normed = normalize(x_float).astype(jnp.bfloat16)
        pre_act = jnp.dot(normed, proj_weight, preferred_element_type=jnp.float32)
        activated = jax.nn.silu(pre_act).astype(jnp.bfloat16)
        query = activated[:, :D].reshape(TOK_G, HEADS, HEAD).astype(jnp.float32)
        keys = activated[:, D:2 * D].reshape(TOK_G, HEADS, HEAD).astype(jnp.float32)
        values = activated[:, 2 * D:].reshape(TOK_G, HEADS, HEAD).astype(jnp.float32)
        places = jnp.arange(TOK_G, dtype=jnp.int32)
        visible = (places[None, :] <= places[:, None]) & (seg_ids[None, :] == seg_ids[:, None])
        scores = jnp.einsum('qhd,khd->hqk', query, keys) * scale
        weights = jnp.where(visible[None], jax.nn.silu(scores) * inv_most, 0.0).astype(jnp.bfloat16)
        attended = jnp.einsum('hqk,khd->qhd', weights.astype(jnp.float32), values).reshape(TOK_G, D)
        output = (x_float + normalize(attended)).astype(jnp.bfloat16)
        grad_att = normalize_back(grad_out.astype(jnp.float32), attended).astype(jnp.bfloat16)
        grad_heads = grad_att.reshape(TOK_G, HEADS, HEAD).astype(jnp.float32)
        grad_prod = jnp.einsum('qhd,khd->hqk', grad_heads, values)
        grad_scores = jnp.where(visible[None], grad_prod * silu_grad(scores) * (inv_most * scale), 0.0).astype(jnp.bfloat16)
        grad_query = jnp.einsum('hqk,khd->qhd', grad_scores.astype(jnp.float32), keys).reshape(TOK_G, D)
        score_parts = grad_scores.astype(jnp.float32).reshape(HEADS, N_CTX, TOK_DEV, TOK_G)
        weight_parts = weights.astype(jnp.float32).reshape(HEADS, N_CTX, TOK_DEV, TOK_G)
        query_parts = query.reshape(N_CTX, TOK_DEV, HEADS, HEAD)
        grad_parts = grad_heads.reshape(N_CTX, TOK_DEV, HEADS, HEAD)
        key_terms = jnp.einsum('hcqk,cqhd->ckhd', score_parts, query_parts).astype(jnp.bfloat16)
        value_terms = jnp.einsum('hcqk,cqhd->ckhd', weight_parts, grad_parts).astype(jnp.bfloat16)
        grad_keys = lax.optimization_barrier(jnp.sum(key_terms.astype(jnp.float32), axis=0)).reshape(TOK_G, D)
        grad_values = lax.optimization_barrier(jnp.sum(value_terms.astype(jnp.float32), axis=0)).reshape(TOK_G, D)
        joined = jnp.concatenate([grad_query, grad_keys, grad_values], axis=1)
        grad_pre = (joined * silu_grad(pre_act)).astype(jnp.bfloat16)
        weight_term = jnp.dot(normed.T, grad_pre, preferred_element_type=jnp.float32)
        grad_normed = jnp.dot(grad_pre, proj_weight.T, preferred_element_type=jnp.float32)
        grad_tok = (grad_out.astype(jnp.float32) + normalize_back(grad_normed, x_float)).astype(jnp.bfloat16)
        return (total + weight_term, (output, grad_tok))
    start = jnp.zeros((D, 3 * D), jnp.float32)
    total, (output, grad_tokens) = lax.scan(one_group, start, (tokens, cotangent, segment))
    return (output, grad_tokens, total * inv_root)
```

```python
import jax
import jax.numpy as jnp
from jax import lax
from jax.experimental import pallas as pl
from jax.experimental.pallas import tpu as pltpu
from jax.sharding import PartitionSpec as P

HEADS = 8
HEAD = 128
EPS = 1e-05
VMEM = 56 * 2**20
F32 = jnp.float32
BF16 = jnp.bfloat16

NN = (((1,), (0,)), ((), ()))
NT = (((1,), (1,)), ((), ()))
TN = (((0,), (0,)), ((), ()))


def dot(a, b, dims=NN):
    return lax.dot_general(a, b, dims, preferred_element_type=F32)


def normalize(value):
    centred = value - jnp.mean(value, axis=-1, keepdims=True)
    spread = jnp.mean(centred * centred, axis=-1, keepdims=True)
    return centred * lax.rsqrt(spread + EPS)


def silu_grad(value):
    half = 0.5 * value
    th = jnp.tanh(half)
    return 0.5 * (1.0 + th) * (1.0 + half * (1.0 - th))


def block_mask(bounds, row0, col0, rows):
    row = row0 + lax.broadcasted_iota(jnp.int32, (rows, 1), 0)
    col = col0 + lax.broadcasted_iota(jnp.int32, (1, rows), 1)
    first = jnp.where(row >= bounds[1], bounds[1], jnp.where(row >= bounds[0], bounds[0], 0))
    return (col <= row) & (col >= first)


def first_block(bounds, row0, rows):
    first = jnp.where(row0 >= bounds[1], bounds[1], jnp.where(row0 >= bounds[0], bounds[0], 0))
    return first // rows


def fwd_kernel(rows, scale, bounds_ref, x_ref, w_ref, cot_ref, normed_ref, pre_ref, act_ref,
               att_ref, stat_ref):
    step = pl.program_id(0)
    bounds = (bounds_ref[0], bounds_ref[1])
    normed = normalize(x_ref[pl.ds(0, rows), :].astype(F32)).astype(BF16)
    normed_ref[...] = normed
    pre = dot(normed, w_ref[...])
    pre_ref[...] = pre
    half = 0.5 * pre
    here = pl.ds(pl.multiple_of(step * rows, rows), rows)
    act_ref[here, :] = (half * (1.0 + jnp.tanh(half))).astype(BF16)
    query = act_ref[here, pl.ds(0, HEAD)]

    def inner(j, total):
        there = pl.ds(pl.multiple_of(j * rows, rows), rows)
        keys = act_ref[there, pl.ds(HEAD, HEAD)]
        values = act_ref[there, pl.ds(2 * HEAD, HEAD)]
        t = dot(query, keys, NT) * (0.5 * scale)
        mask = block_mask(bounds, step * rows, j * rows, rows)
        weights = jnp.where(mask, t * (1.0 + jnp.tanh(t)), 0.0).astype(BF16)
        return total + dot(weights, values)

    att = lax.fori_loop(
        first_block(bounds, step * rows, rows), step + 1, inner, jnp.zeros((rows, HEAD), F32)
    ) * (1.0 / 1024)
    att_t = att.T
    att_ref[...] = att_t
    cot_t = cot_ref[...].astype(F32).T
    mean = jnp.mean(att_t, axis=0, keepdims=True)
    centred = att_t - mean
    stat_ref[...] = jnp.concatenate(
        [
            mean,
            jnp.sum(centred * centred, axis=0, keepdims=True),
            jnp.sum(cot_t * centred, axis=0, keepdims=True),
            jnp.sum(cot_t, axis=0, keepdims=True),
            jnp.zeros((4, rows), F32),
        ],
        axis=0,
    )


def bwd_kernel(rows, scale, inv_root, bounds_ref, act_ref, att_ref, cot_ref, stat_ref, normed_ref,
               pre_ref, out_ref, gw_ref, n_s, dq_s, dk_s, dv_s, gw_s):
    step = pl.program_id(0)
    steps = pl.num_programs(0) // 2
    bounds = (bounds_ref[0], bounds_ref[1])
    width = HEADS * HEAD

    @pl.when(step < steps)
    def _():
        stat = stat_ref[...].reshape(HEADS, 8, rows)
        means, second, cross, sums = stat[:, 0], stat[:, 1], stat[:, 2], stat[:, 3]
        mean = jnp.mean(means, axis=0, keepdims=True)
        shift = means - mean
        var = jnp.sum(second + HEAD * shift * shift, axis=0, keepdims=True) * (1.0 / width)
        factor = lax.rsqrt(var + EPS)
        mean_cot = jnp.sum(sums, axis=0, keepdims=True) * (1.0 / width)
        inner_mean = factor * jnp.sum(cross + shift * sums, axis=0, keepdims=True) * (1.0 / width)
        n_t = (att_ref[...] - mean) * factor
        cot_t = cot_ref[...].astype(F32).T
        ga_t = factor * (cot_t - mean_cot - n_t * inner_mean)
        here = pl.ds(pl.multiple_of(step * rows, rows), rows)
        n_s[here, :] = n_t.T.astype(BF16)
        grad_att = ga_t.T.astype(BF16)
        ga_tb = ga_t.astype(BF16)
        query = act_ref[here, pl.ds(0, HEAD)]
        query_t = query.astype(F32).T.astype(BF16)
        dk_s[step] = jnp.zeros((HEAD, rows), F32)
        dv_s[step] = jnp.zeros((HEAD, rows), F32)

        def inner(j, total):
            there = pl.ds(pl.multiple_of(j * rows, rows), rows)
            keys = act_ref[there, pl.ds(HEAD, HEAD)]
            values = act_ref[there, pl.ds(2 * HEAD, HEAD)]
            t = dot(query, keys, NT) * (0.5 * scale)
            prod = dot(grad_att, values, NT)
            mask = block_mask(bounds, step * rows, j * rows, rows)
            th = jnp.tanh(t)
            up = 1.0 + th
            weights = jnp.where(mask, t * up, 0.0).astype(BF16)
            grads = jnp.where(mask, prod * (up * (1.0 + t * (1.0 - th))), 0.0).astype(BF16)
            dv_s[j] += dot(ga_tb, weights)
            dk_s[j] += dot(query_t, grads)
            return total + dot(grads, keys)

        dq_s[here, :] = lax.fori_loop(
            first_block(bounds, step * rows, rows), step + 1, inner, jnp.zeros((rows, HEAD), F32)
        )

    @pl.when(step >= steps)
    def _():
        block = step - steps
        here = pl.ds(pl.multiple_of(block * rows, rows), rows)
        slope = silu_grad(pre_ref[...])
        inv = 1.0 / 1024
        gpre = jnp.concatenate(
            [
                dq_s[here, :] * (0.5 * inv * scale),
                dk_s[block].T * (0.5 * inv * scale),
                dv_s[block].T * inv,
            ],
            axis=1,
        )
        gpre = (gpre * slope).astype(BF16)
        out_ref[:, pl.ds(0, HEAD)] = n_s[here, :]
        out_ref[:, pl.ds(HEAD, 3 * HEAD)] = gpre
        term = dot(normed_ref[...], gpre, TN)

        @pl.when(block == 0)
        def _():
            gw_s[...] = term

        @pl.when(block > 0)
        def _():
            gw_s[...] += term

        @pl.when(block == steps - 1)
        def _():
            gw_ref[...] = (gw_s[...] * inv_root).astype(BF16)


def out_kernel(rows, got_ref, w_ref, x_ref, cot_ref, out_ref, gtok_ref, g_s, acc_s):
    step = pl.program_id(0)
    width = HEADS * HEAD
    part = w_ref.shape[0]

    @pl.when(step == 0)
    def _():
        for h in range(HEADS):
            out_ref[:, pl.ds(h * HEAD, HEAD)] = (
                x_ref[:, pl.ds(h * HEAD, HEAD)].astype(F32)
                + got_ref[h, :, pl.ds(0, HEAD)].astype(F32)
            ).astype(BF16)
            for t in range(3):
                g_s[:, pl.ds(t * width + h * HEAD, HEAD)] = got_ref[h, :, pl.ds((t + 1) * HEAD, HEAD)]

    acc_s[step] = dot(g_s[...], w_ref[...], NT)

    @pl.when(step == pl.num_programs(0) - 1)
    def _():
        x = x_ref[...].astype(F32)
        centred = x - jnp.mean(x, axis=-1, keepdims=True)
        factor = lax.rsqrt(jnp.mean(centred * centred, axis=-1, keepdims=True) + EPS)
        normal = centred * factor
        grad = jnp.concatenate([acc_s[i] for i in range(width // part)], axis=1)
        back = factor * (
            grad
            - jnp.mean(grad, axis=-1, keepdims=True)
            - normal * jnp.mean(grad * normal, axis=-1, keepdims=True)
        )
        gtok_ref[...] = (cot_ref[...].astype(F32) + back).astype(BF16)


def join_kernel(got_ref, out_ref):
    for h in range(HEADS):
        for t in range(3):
            out_ref[:, pl.ds((t * HEADS + h) * HEAD, HEAD)] = got_ref[
                h, :, pl.ds(t * HEAD, HEAD)
            ].astype(F32)


def params(n):
    return pltpu.CompilerParams(dimension_semantics=("arbitrary",) * n, vmem_limit_bytes=VMEM)


def body(tokens, cotangent, proj_weight, segment):
    x_tok = tokens[0]
    grad_out = cotangent[0]
    seg_ids = segment[0]
    rows, width = x_tok.shape
    ctx_count = lax.axis_size("ctx")
    dp_count = lax.axis_size("dp")
    total = rows * ctx_count
    scale = 1.0 / HEAD**0.5
    inv_root = 1.0 / (dp_count * total) ** 0.5
    head = lax.axis_index("ctx")

    seg_row = jnp.pad(seg_ids.astype(BF16)[None, :], ((0, 15), (0, width - rows)))
    sent = jnp.concatenate([x_tok, seg_row], axis=0)
    shard = sent.shape[0]
    got = lax.all_gather(sent, "ctx", axis=0, tiled=True)
    cot_head = lax.all_to_all(
        grad_out.reshape(rows, HEADS, HEAD).transpose(1, 0, 2), "ctx", 0, 0
    ).reshape(total, HEAD)
    all_seg = got.reshape(ctx_count, shard, width)[:, rows, :rows].astype(F32)
    bounds = jnp.stack([jnp.sum(all_seg < 0.5), jnp.sum(all_seg < 1.5)]).astype(jnp.int32)

    w_head = jnp.concatenate(
        [lax.dynamic_slice_in_dim(proj_weight, t * width + head * HEAD, HEAD, 1) for t in range(3)],
        axis=1,
    )
    normed, pre, act, att_t, stat = pl.pallas_call(
        lambda *refs: fwd_kernel(rows, scale, *refs),
        grid_spec=pltpu.PrefetchScalarGridSpec(
            num_scalar_prefetch=1,
            grid=(ctx_count,),
            in_specs=[
                pl.BlockSpec((shard, width), lambda i, b: (i, 0)),
                pl.BlockSpec((width, 3 * HEAD), lambda i, b: (0, 0)),
                pl.BlockSpec((rows, HEAD), lambda i, b: (i, 0)),
            ],
            out_specs=[
                pl.BlockSpec((rows, width), lambda i, b: (i, 0)),
                pl.BlockSpec((rows, 3 * HEAD), lambda i, b: (i, 0)),
                pl.BlockSpec((total, 3 * HEAD), lambda i, b: (0, 0)),
                pl.BlockSpec((HEAD, rows), lambda i, b: (0, i)),
                pl.BlockSpec((8, rows), lambda i, b: (0, i)),
            ],
        ),
        out_shape=[
            jax.ShapeDtypeStruct((total, width), BF16),
            jax.ShapeDtypeStruct((total, 3 * HEAD), F32),
            jax.ShapeDtypeStruct((total, 3 * HEAD), BF16),
            jax.ShapeDtypeStruct((HEAD, total), F32),
            jax.ShapeDtypeStruct((8, total), F32),
        ],
        compiler_params=params(1),
        name="attend",
    )(bounds, got, w_head, cot_head)

    all_stat = lax.all_gather(stat, "ctx", axis=0, tiled=True)

    late = lambda i: jnp.maximum(i - ctx_count, 0)
    early = lambda i: jnp.minimum(i, ctx_count - 1)
    back, gw = pl.pallas_call(
        lambda *refs: bwd_kernel(rows, scale, inv_root, *refs),
        grid_spec=pltpu.PrefetchScalarGridSpec(
            num_scalar_prefetch=1,
            grid=(2 * ctx_count,),
            in_specs=[
                pl.BlockSpec((total, 3 * HEAD), lambda i, b: (0, 0)),
                pl.BlockSpec((HEAD, rows), lambda i, b: (0, early(i))),
                pl.BlockSpec((rows, HEAD), lambda i, b: (early(i), 0)),
                pl.BlockSpec((8 * HEADS, rows), lambda i, b: (0, early(i))),
                pl.BlockSpec((rows, width), lambda i, b: (late(i), 0)),
                pl.BlockSpec((rows, 3 * HEAD), lambda i, b: (late(i), 0)),
            ],
            out_specs=[
                pl.BlockSpec((rows, 4 * HEAD), lambda i, b: (late(i), 0)),
                pl.BlockSpec((width, 3 * HEAD), lambda i, b: (0, 0)),
            ],
            scratch_shapes=[
                pltpu.VMEM((total, HEAD), BF16),
                pltpu.VMEM((total, HEAD), F32),
                pltpu.VMEM((ctx_count, HEAD, rows), F32),
                pltpu.VMEM((ctx_count, HEAD, rows), F32),
                pltpu.VMEM((width, 3 * HEAD), F32),
            ],
        ),
        out_shape=[
            jax.ShapeDtypeStruct((total, 4 * HEAD), BF16),
            jax.ShapeDtypeStruct((width, 3 * HEAD), BF16),
        ],
        compiler_params=params(1),
        name="attend_back",
    )(bounds, act, att_t, cot_head, all_stat, normed, pre)

    piece = width // dp_count
    terms = lax.all_to_all(gw.reshape(dp_count, piece, 3 * HEAD), "dp", 0, 0)
    summed = jnp.sum(terms.astype(F32), axis=0).astype(BF16)
    pieces = lax.all_gather(summed, ("dp", "ctx"), axis=0, tiled=False)
    grad_weight = pl.pallas_call(
        join_kernel,
        grid=(dp_count,),
        in_specs=[pl.BlockSpec((ctx_count, piece, 3 * HEAD), lambda i: (i, 0, 0))],
        out_specs=pl.BlockSpec((piece, 3 * width), lambda i: (i, 0)),
        out_shape=jax.ShapeDtypeStruct((width, 3 * width), F32),
        compiler_params=params(1),
        name="join",
    )(pieces)

    mine = lax.all_to_all(back.reshape(ctx_count, rows, 4 * HEAD), "ctx", 0, 0)
    part = 256
    output, grad_tok = pl.pallas_call(
        lambda *refs: out_kernel(rows, *refs),
        grid=(width // part,),
        in_specs=[
            pl.BlockSpec((HEADS, rows, 4 * HEAD), lambda i: (0, 0, 0)),
            pl.BlockSpec((part, 3 * width), lambda i: (i, 0)),
            pl.BlockSpec((rows, width), lambda i: (0, 0)),
            pl.BlockSpec((rows, width), lambda i: (0, 0)),
        ],
        out_specs=[
            pl.BlockSpec((rows, width), lambda i: (0, 0)),
            pl.BlockSpec((rows, width), lambda i: (0, 0)),
        ],
        out_shape=[jax.ShapeDtypeStruct((rows, width), BF16)] * 2,
        scratch_shapes=[
            pltpu.VMEM((rows, 3 * width), BF16),
            pltpu.VMEM((width // part, rows, part), F32),
        ],
        compiler_params=params(1),
        name="finish",
    )(mine, proj_weight, x_tok, grad_out)
    return (output[None], grad_tok[None], grad_weight)


def solution(mesh):
    in_specs = (P("dp", "ctx", None), P("dp", "ctx", None), P(), P("dp", "ctx"))
    out_specs = (P("dp", "ctx", None), P("dp", "ctx", None), P())
    return jax.shard_map(body, mesh=mesh, in_specs=in_specs, out_specs=out_specs, check_vma=False)
```

```python
import jax
import jax.numpy as jnp
from jax import lax
from jax.experimental import pallas as pl
from jax.experimental.pallas import tpu as pltpu
from jax.sharding import PartitionSpec as P

HEADS = 8
HEAD = 128
EPS = 1e-05
VMEM = 56 * 2**20
F32 = jnp.float32
BF16 = jnp.bfloat16

NN = (((1,), (0,)), ((), ()))
NT = (((1,), (1,)), ((), ()))
TN = (((0,), (0,)), ((), ()))


def dot(a, b, dims=NN):
    return lax.dot_general(a, b, dims, preferred_element_type=F32)


def normalize(value):
    centred = value - jnp.mean(value, axis=-1, keepdims=True)
    spread = jnp.mean(centred * centred, axis=-1, keepdims=True)
    return centred * lax.rsqrt(spread + EPS)


def silu_grad(value):
    half = 0.5 * value
    th = jnp.tanh(half)
    return 0.5 * (1.0 + th) * (1.0 + half * (1.0 - th))


def history_start(bounds, row):
    return jnp.where(row >= bounds[1], bounds[1], jnp.where(row >= bounds[0], bounds[0], 0))


def proj_kernel(order_ref, x_ref, w_ref, *refs):
    normed_ref, pre_ref, act_ref = refs[-3:]
    normed = normalize(x_ref[0].astype(F32)).astype(BF16)
    normed_ref[...] = normed
    pre = dot(normed, w_ref[...])
    pre_ref[...] = pre
    half = 0.5 * pre
    act_ref[...] = (half * (1.0 + jnp.tanh(half))).astype(BF16)


def fwd_kernel(rows, scale, place_ref, bounds_ref, act_ref, cot_ref, att_ref, stat_ref):
    step = pl.program_id(0)
    bounds = (bounds_ref[0], bounds_ref[1])
    here = pl.ds(pl.multiple_of(step * rows, rows), rows)
    query = act_ref[here, pl.ds(0, HEAD)]
    wide = 2 * rows
    end = (step + 1) * rows
    row = step * rows + lax.broadcasted_iota(jnp.int32, (rows, 1), 0)
    first = history_start(bounds, row)

    def inner(p, total):
        col0 = pl.multiple_of(jnp.maximum(end - (p + 1) * wide, 0), rows)
        there = pl.ds(col0, wide)
        keys = act_ref[there, pl.ds(HEAD, HEAD)]
        values = act_ref[there, pl.ds(2 * HEAD, HEAD)]
        t = dot(query, keys, NT) * (0.5 * scale)
        col = col0 + lax.broadcasted_iota(jnp.int32, (1, wide), 1)
        last = jnp.minimum(row, end - p * wide - 1)
        mask = (col <= last) & (col >= first)
        weights = jnp.where(mask, t * (1.0 + jnp.tanh(t)), 0.0).astype(BF16)
        return total + dot(weights, values)

    count = (end - history_start(bounds, step * rows) + wide - 1) // wide
    att = lax.fori_loop(0, count, inner, jnp.zeros((rows, HEAD), F32)) * (1.0 / 1024)
    att_t = att.T
    att_ref[...] = att_t
    cot_t = cot_ref[0].astype(F32).T
    mean = jnp.mean(att_t, axis=0, keepdims=True)
    centred = att_t - mean
    stat_ref[...] = jnp.concatenate(
        [
            mean,
            jnp.sum(centred * centred, axis=0, keepdims=True),
            jnp.sum(cot_t * centred, axis=0, keepdims=True),
            jnp.sum(cot_t, axis=0, keepdims=True),
        ],
        axis=0,
    )


def bwd_kernel(rows, scale, inv_root, place_ref, bounds_ref, act_ref, att_ref, cot_ref, stat0_ref,
               stat1_ref, stat2_ref, stat3_ref, normed_ref, pre_ref, out_ref, gw_ref, n_s, dq_s, dk_s,
               dv_s, gw_s):
    step = pl.program_id(0)
    steps = pl.num_programs(0) // 2
    bounds = (bounds_ref[0], bounds_ref[1])
    width = HEADS * HEAD

    @pl.when(step < steps)
    def _():
        stats = [ref[...] for ref in (stat0_ref, stat1_ref, stat2_ref, stat3_ref)]
        means, second, cross, sums = (
            jnp.concatenate([s[r + i : r + i + 1] for s in stats for r in (0, 4)], axis=0)
            for i in range(4)
        )
        mean = jnp.mean(means, axis=0, keepdims=True)
        shift = means - mean
        var = jnp.sum(second + HEAD * shift * shift, axis=0, keepdims=True) * (1.0 / width)
        factor = lax.rsqrt(var + EPS)
        mean_cot = jnp.sum(sums, axis=0, keepdims=True) * (1.0 / width)
        inner_mean = factor * jnp.sum(cross + shift * sums, axis=0, keepdims=True) * (1.0 / width)
        n_t = (att_ref[...] - mean) * factor
        cot_t = cot_ref[0].astype(F32).T
        ga_t = factor * (cot_t - mean_cot - n_t * inner_mean)
        here = pl.ds(pl.multiple_of(step * rows, rows), rows)
        n_s[here, :] = n_t.T.astype(BF16)
        grad_att = ga_t.T.astype(BF16)
        ga_tb = ga_t.astype(BF16)
        query = act_ref[here, pl.ds(0, HEAD)]
        query_t = query.astype(F32).T.astype(BF16)
        row = step * rows + lax.broadcasted_iota(jnp.int32, (rows, 1), 0)
        first = history_start(bounds, row)
        dk_s[step] = jnp.zeros((HEAD, rows), F32)
        dv_s[step] = jnp.zeros((HEAD, rows), F32)

        def inner(j, total):
            there = pl.ds(pl.multiple_of(j * rows, rows), rows)
            keys = act_ref[there, pl.ds(HEAD, HEAD)]
            values = act_ref[there, pl.ds(2 * HEAD, HEAD)]
            t = dot(query, keys, NT) * (0.5 * scale)
            prod = dot(grad_att, values, NT)
            col = j * rows + lax.broadcasted_iota(jnp.int32, (1, rows), 1)
            mask = (col <= row) & (col >= first)
            th = jnp.tanh(t)
            up = 1.0 + th
            weights = jnp.where(mask, t * up, 0.0).astype(BF16)
            grads = jnp.where(mask, prod * (up * (1.0 + t * (1.0 - th))), 0.0).astype(BF16)
            dv_s[j] += dot(ga_tb, weights)
            dk_s[j] += dot(query_t, grads)
            return total + dot(grads, keys)

        dq_s[here, :] = lax.fori_loop(
            history_start(bounds, step * rows) // rows, step + 1, inner, jnp.zeros((rows, HEAD), F32)
        )

    @pl.when(step >= steps)
    def _():
        block = step - steps
        here = pl.ds(pl.multiple_of(block * rows, rows), rows)
        slope = silu_grad(pre_ref[...])
        inv = 1.0 / 1024
        gpre = jnp.concatenate(
            [
                dq_s[here, :] * (0.5 * inv * scale),
                dk_s[block].T * (0.5 * inv * scale),
                dv_s[block].T * inv,
            ],
            axis=1,
        )
        gpre = (gpre * slope).astype(BF16)
        out_ref[:, pl.ds(0, HEAD)] = n_s[here, :]
        out_ref[:, pl.ds(HEAD, 3 * HEAD)] = gpre
        term = dot(normed_ref[...], gpre, TN)

        @pl.when(block == 0)
        def _():
            gw_s[...] = term

        @pl.when(block > 0)
        def _():
            gw_s[...] += term

        @pl.when(block == steps - 1)
        def _():
            gw_ref[...] = (gw_s[...] * inv_root).astype(BF16)


def out_kernel(rows, heads_ref, got0_ref, got1_ref, got2_ref, got3_ref, w_ref, x_ref, cot_ref,
               out_ref, gtok_ref, g_s, acc_s):
    step = pl.program_id(0)
    width = HEADS * HEAD
    part = w_ref.shape[0]

    @pl.when(step == 0)
    def _():
        for s, got_ref in enumerate((got0_ref, got1_ref, got2_ref, got3_ref)):
            for j in range(2):
                col = pl.multiple_of(heads_ref[2 * s + j] * HEAD, HEAD)
                out_ref[:, pl.ds(col, HEAD)] = (
                    x_ref[:, pl.ds(col, HEAD)].astype(F32) + got_ref[j, :, pl.ds(0, HEAD)].astype(F32)
                ).astype(BF16)
                for t in range(3):
                    g_s[:, pl.ds(t * width + col, HEAD)] = got_ref[j, :, pl.ds((t + 1) * HEAD, HEAD)]

    acc_s[step] = dot(g_s[...], w_ref[...], NT)

    @pl.when(step == pl.num_programs(0) - 1)
    def _():
        x = x_ref[...].astype(F32)
        centred = x - jnp.mean(x, axis=-1, keepdims=True)
        factor = lax.rsqrt(jnp.mean(centred * centred, axis=-1, keepdims=True) + EPS)
        normal = centred * factor
        grad = jnp.concatenate([acc_s[i] for i in range(width // part)], axis=1)
        back = factor * (
            grad
            - jnp.mean(grad, axis=-1, keepdims=True)
            - normal * jnp.mean(grad * normal, axis=-1, keepdims=True)
        )
        gtok_ref[...] = (cot_ref[...].astype(F32) + back).astype(BF16)


def join_kernel(piece, where_ref, *refs):
    same, other = refs[:4], refs[4:8]
    out_ref, buf, sem = refs[8:]
    step = pl.program_id(0)

    def fetch(q, wait):
        for side, group in enumerate((same, other)):
            rel = lax.rem(q - where_ref[side] + 4, 4)
            slot = lax.rem(q, 2)
            for a, ref in enumerate(group):

                @pl.when(rel == a)
                def _():
                    copy = pltpu.make_async_copy(ref, buf.at[slot, side], sem.at[slot, side])
                    copy.wait() if wait else copy.start()

    @pl.when(step == 0)
    def _():
        fetch(step, False)

    @pl.when(step + 1 < pl.num_programs(0))
    def _():
        fetch(step + 1, False)

    fetch(step, True)
    slot = lax.rem(step, 2)
    for side in range(2):
        for s in range(4):
            head = where_ref[2 + 4 * side + s]
            for t in range(3):
                col = pl.multiple_of((t * HEADS + head) * HEAD, HEAD)
                out_ref[:, pl.ds(col, HEAD)] = buf[slot, side, s, :, pl.ds(t * HEAD, HEAD)].astype(F32)


def params(n):
    return pltpu.CompilerParams(dimension_semantics=("arbitrary",) * n, vmem_limit_bytes=VMEM)


SIDE = 4


def ring(axis, step):
    pairs = []
    for place in range(2 * SIDE**3):
        core = place % 2
        at = [place // (2 * SIDE * SIDE), place // (2 * SIDE) % SIDE, place // 2 % SIDE]
        at[axis(core)] = (at[axis(core)] + step) % SIDE
        pairs.append((place, ((at[0] * SIDE + at[1]) * SIDE + at[2]) * 2 + core))
    return pairs


def along(axis):
    return lambda value, step: lax.ppermute(value, ("dp", "ctx"), ring(axis, step))


def along_z(value, step):
    return lax.ppermute(value, "ctx", [(c, (c + 2 * step) % 8) for c in range(8)])


def swap(value):
    return lax.ppermute(value, "ctx", [(c, c ^ 1) for c in range(8)])


def to_head(chunks, core, z):
    pairs = chunks.reshape((SIDE, 2) + chunks.shape[1:])
    pick = lambda a, i, dim: lax.dynamic_index_in_dim(a, i, dim, keepdims=False)
    mine = pick(pairs, core, 1)
    theirs = swap(pick(pairs, 1 - core, 1))
    send = lambda d: jnp.stack([pick(mine, (z + d) % SIDE, 0), pick(theirs, (z + d) % SIDE, 0)])
    far, after, before = (along_z(send(d), d) for d in (2, 1, -1))
    return send(0), after, before, far


def body(tokens, cotangent, proj_weight, segment):
    x_tok = tokens[0]
    grad_out = cotangent[0]
    seg_ids = segment[0]
    rows, width = x_tok.shape
    ctx_count = lax.axis_size("ctx")
    dp_count = lax.axis_size("dp")
    total = rows * ctx_count
    scale = 1.0 / HEAD**0.5
    inv_root = 1.0 / (dp_count * total) ** 0.5
    head = lax.axis_index("ctx")
    core, z = head % 2, head // 2
    x_at, y_at = lax.axis_index("dp") // SIDE, lax.axis_index("dp") % SIDE
    near = jnp.stack([head, (head + 6) % 8, (head + 2) % 8, (head + 4) % 8])
    order = jnp.stack([near, near ^ 1], axis=1).reshape(8).astype(jnp.int32)
    place = jnp.sum(
        jnp.where(order[:, None] == jnp.arange(8)[None, :], jnp.arange(8)[:, None], 0), axis=0
    ).astype(jnp.int32)

    before = along_z(x_tok, 1)
    after = along_z(x_tok, -1)
    partner = swap(x_tok)
    counts = jnp.stack([jnp.sum(seg_ids < 1), jnp.sum(seg_ids < 2)]).astype(F32)
    counts = jnp.broadcast_to(counts[:, None], (2, HEAD))
    counts = counts + swap(counts)
    counts = (counts + along_z(counts, 2)) + (along_z(counts, 1) + along_z(counts, -1))
    bounds = counts[:, 0].astype(jnp.int32)
    half = rows // 2
    far_low = along_z(before[:half], 1)
    far_high = along_z(after[half:], -1)
    w_head = jnp.concatenate(
        [lax.dynamic_slice_in_dim(proj_weight, t * width + head * HEAD, HEAD, 1) for t in range(3)],
        axis=1,
    )
    cot_chunks = grad_out.reshape(rows, HEADS, HEAD).transpose(1, 0, 2)
    cot_head = jnp.concatenate(to_head(cot_chunks, core, z), axis=0)

    def project(count, first, shards, earlier):
        return pl.pallas_call(
            proj_kernel,
            grid_spec=pltpu.PrefetchScalarGridSpec(
                num_scalar_prefetch=1,
                grid=(count,),
                in_specs=[
                    pl.BlockSpec((1, rows, width), lambda i, o: (i, 0, 0)),
                    pl.BlockSpec((width, 3 * HEAD), lambda i, o: (0, 0)),
                ]
                + [pl.BlockSpec(memory_space=pl.ANY)] * len(earlier),
                out_specs=[
                    pl.BlockSpec((rows, width), lambda i, o: (o[first + i], 0)),
                    pl.BlockSpec((rows, 3 * HEAD), lambda i, o: (o[first + i], 0)),
                    pl.BlockSpec((rows, 3 * HEAD), lambda i, o: (o[first + i], 0)),
                ],
            ),
            out_shape=[
                jax.ShapeDtypeStruct((total, width), BF16),
                jax.ShapeDtypeStruct((total, 3 * HEAD), F32),
                jax.ShapeDtypeStruct((total, 3 * HEAD), BF16),
            ],
            input_output_aliases={3 + i: i for i in range(len(earlier))},
            compiler_params=params(1),
            cost_estimate=pl.CostEstimate(
                flops=count * 2 * rows * width * 3 * HEAD,
                bytes_accessed=count * rows * width * 6,
                transcendentals=0,
            ),
            name="project",
        )(order, shards, w_head, *earlier)

    seen = project(
        6, 0, jnp.stack([x_tok, partner, before, swap(before), after, swap(after)]), ()
    )
    far = jnp.concatenate([far_low, far_high], axis=0)
    far_other = jnp.concatenate([swap(far_low), swap(far_high)], axis=0)
    normed, pre, act = project(2, 6, jnp.stack([far, far_other]), seen)

    att_t, stat = pl.pallas_call(
        lambda *refs: fwd_kernel(rows, scale, *refs),
        grid_spec=pltpu.PrefetchScalarGridSpec(
            num_scalar_prefetch=2,
            grid=(ctx_count,),
            in_specs=[
                pl.BlockSpec((total, 3 * HEAD), lambda i, p, b: (0, 0)),
                pl.BlockSpec((1, rows, HEAD), lambda i, p, b: (p[i], 0, 0)),
            ],
            out_specs=[
                pl.BlockSpec((HEAD, rows), lambda i, p, b: (0, i)),
                pl.BlockSpec((4, rows), lambda i, p, b: (0, i)),
            ],
        ),
        out_shape=[
            jax.ShapeDtypeStruct((HEAD, total), F32),
            jax.ShapeDtypeStruct((4, total), F32),
        ],
        compiler_params=params(1),
        name="attend",
    )(place, bounds, act, cot_head)

    pair = jnp.concatenate([stat, swap(stat)], axis=0)
    stats = (pair, along_z(pair, 2), along_z(pair, 1), along_z(pair, -1))

    late = lambda i: jnp.maximum(i - ctx_count, 0)
    early = lambda i: jnp.minimum(i, ctx_count - 1)
    back, gw = pl.pallas_call(
        lambda *refs: bwd_kernel(rows, scale, inv_root, *refs),
        grid_spec=pltpu.PrefetchScalarGridSpec(
            num_scalar_prefetch=2,
            grid=(2 * ctx_count,),
            in_specs=[
                pl.BlockSpec((total, 3 * HEAD), lambda i, p, b: (0, 0)),
                pl.BlockSpec((HEAD, rows), lambda i, p, b: (0, early(i))),
                pl.BlockSpec((1, rows, HEAD), lambda i, p, b: (p[early(i)], 0, 0)),
            ]
            + [pl.BlockSpec((8, rows), lambda i, p, b: (0, early(i)))] * 4
            + [
                pl.BlockSpec((rows, width), lambda i, p, b: (late(i), 0)),
                pl.BlockSpec((rows, 3 * HEAD), lambda i, p, b: (late(i), 0)),
            ],
            out_specs=[
                pl.BlockSpec((rows, 4 * HEAD), lambda i, p, b: (late(i), 0)),
                pl.BlockSpec((width, 3 * HEAD), lambda i, p, b: (0, 0)),
            ],
            scratch_shapes=[
                pltpu.VMEM((total, HEAD), BF16),
                pltpu.VMEM((total, HEAD), F32),
                pltpu.VMEM((ctx_count, HEAD, rows), F32),
                pltpu.VMEM((ctx_count, HEAD, rows), F32),
                pltpu.VMEM((width, 3 * HEAD), F32),
            ],
        ),
        out_shape=[
            jax.ShapeDtypeStruct((total, 4 * HEAD), BF16),
            jax.ShapeDtypeStruct((width, 3 * HEAD), BF16),
        ],
        compiler_params=params(1),
        name="attend_back",
    )(place, bounds, act, att_t, cot_head, *stats, normed, pre)

    first_way = along(lambda c: c)
    other_way = along(lambda c: 1 - c)
    piece = width // SIDE
    my_piece = jnp.where(core == 0, x_at, y_at)
    cut = lambda d: lax.dynamic_slice_in_dim(gw, (my_piece + d) % SIDE * piece, piece, 0)
    up = lambda v: v.astype(F32)
    terms = [first_way(cut(d), d) for d in (2, 1, -1)]
    summed = ((up(cut(0)) + up(terms[0])) + (up(terms[1]) + up(terms[2]))).astype(BF16)
    terms = [other_way(summed, d) for d in (2, 1, -1)]
    summed = ((up(summed) + up(terms[0])) + (up(terms[1]) + up(terms[2]))).astype(BF16)
    chips = jnp.stack([summed, along_z(summed, 1), along_z(summed, -1), along_z(summed, 2)])
    same = [chips, first_way(chips, -1), first_way(chips, 2), first_way(chips, 1)]
    other = [swap(v) for v in same]
    z_order = jnp.stack([z, (z + 3) % SIDE, (z + 1) % SIDE, (z + 2) % SIDE])
    where = jnp.concatenate(
        [
            jnp.stack([my_piece, jnp.where(core == 0, y_at, x_at)]),
            2 * z_order + core,
            2 * z_order + 1 - core,
        ]
    ).astype(jnp.int32)
    grad_weight = pl.pallas_call(
        lambda *refs: join_kernel(piece, *refs),
        grid_spec=pltpu.PrefetchScalarGridSpec(
            num_scalar_prefetch=1,
            grid=(SIDE,),
            in_specs=[pl.BlockSpec(memory_space=pl.ANY)] * 8,
            out_specs=pl.BlockSpec((piece, 3 * width), lambda i, w: (i, 0)),
            scratch_shapes=[
                pltpu.VMEM((2, 2, SIDE, piece, 3 * HEAD), BF16),
                pltpu.SemaphoreType.DMA((2, 2)),
            ],
        ),
        out_shape=jax.ShapeDtypeStruct((width, 3 * width), F32),
        compiler_params=params(1),
        name="join",
    )(where, *same, *other)

    mine = to_head(back.reshape(ctx_count, rows, 4 * HEAD), core, z)
    part = 256
    output, grad_tok = pl.pallas_call(
        lambda *refs: out_kernel(rows, *refs),
        grid_spec=pltpu.PrefetchScalarGridSpec(
            num_scalar_prefetch=1,
            grid=(width // part,),
            in_specs=[pl.BlockSpec((2, rows, 4 * HEAD), lambda i, o: (0, 0, 0))] * 4
            + [
                pl.BlockSpec((part, 3 * width), lambda i, o: (i, 0)),
                pl.BlockSpec((rows, width), lambda i, o: (0, 0)),
                pl.BlockSpec((rows, width), lambda i, o: (0, 0)),
            ],
            out_specs=[
                pl.BlockSpec((rows, width), lambda i, o: (0, 0)),
                pl.BlockSpec((rows, width), lambda i, o: (0, 0)),
            ],
            scratch_shapes=[
                pltpu.VMEM((rows, 3 * width), BF16),
                pltpu.VMEM((width // part, rows, part), F32),
            ],
        ),
        out_shape=[jax.ShapeDtypeStruct((rows, width), BF16)] * 2,
        compiler_params=params(1),
        cost_estimate=pl.CostEstimate(
            flops=2 * rows * width * 3 * width, bytes_accessed=10 * 2**20, transcendentals=0
        ),
        name="finish",
    )(order, *mine, proj_weight, x_tok, grad_out)
    return (output[None], grad_tok[None], grad_weight)


def solution(mesh):
    in_specs = (P("dp", "ctx", None), P("dp", "ctx", None), P(), P("dp", "ctx"))
    out_specs = (P("dp", "ctx", None), P("dp", "ctx", None), P())
    return jax.shard_map(body, mesh=mesh, in_specs=in_specs, out_specs=out_specs, check_vma=False)
```

```python
import jax
import jax.numpy as jnp
from jax import lax
from jax.experimental import pallas as pl
from jax.experimental.pallas import tpu as pltpu
from jax.sharding import PartitionSpec as P

HEADS = 8
HEAD = 128
EPS = 1e-05
VMEM = 56 * 2**20
F32 = jnp.float32
BF16 = jnp.bfloat16

NN = (((1,), (0,)), ((), ()))
NT = (((1,), (1,)), ((), ()))
TN = (((0,), (0,)), ((), ()))


def dot(a, b, dims=NN):
    return lax.dot_general(a, b, dims, preferred_element_type=F32)


def normalize(value):
    centred = value - jnp.mean(value, axis=-1, keepdims=True)
    spread = jnp.mean(centred * centred, axis=-1, keepdims=True)
    return centred * lax.rsqrt(spread + EPS)


def silu_grad(value):
    half = 0.5 * value
    th = jnp.tanh(half)
    return 0.5 * (1.0 + th) * (1.0 + half * (1.0 - th))


def history_start(bounds, row):
    return jnp.where(row >= bounds[1], bounds[1], jnp.where(row >= bounds[0], bounds[0], 0))


def proj_kernel(rows, starts, at_ref, *refs):
    count = len(starts)
    x_refs, w_ref = refs[:count], refs[count]
    normed_ref, pre_ref, act_ref, token_ref = refs[-4:]
    token_ref[...] = jnp.zeros_like(token_ref)
    for (other, start), x_ref in zip(starts, x_refs):
        size = x_ref.shape[0]
        core = 1 - at_ref[1] if other else at_ref[1]
        here = pl.ds(pl.multiple_of(core * rows + start, size), size)
        normed = normalize(x_ref[...].astype(F32)).astype(BF16)
        normed_ref[here, :] = normed
        pre = dot(normed, w_ref[...])
        pre_ref[here, :] = pre
        half = 0.5 * pre
        act_ref[here, :] = (half * (1.0 + jnp.tanh(half))).astype(BF16)


def fwd_kernel(rows, scale, order_ref, bounds_ref, act_ref, *refs):
    got_refs, (att_ref, stat_ref, cot_ref) = refs[:4], refs[4:]
    bounds = (bounds_ref[0], bounds_ref[1])
    wide = 2 * rows
    for s in range(2 * len(got_refs)):
        there = pl.ds(pl.multiple_of(order_ref[s] * rows, rows), rows)
        cot_ref[there, :] = got_refs[s // 2][s % 2, pl.ds(0, rows), :]

    def block(i, carry):
        row0 = pl.multiple_of(i * rows, rows)
        here = pl.ds(row0, rows)
        query = act_ref[here, pl.ds(0, HEAD)]
        end = row0 + rows
        row = row0 + lax.broadcasted_iota(jnp.int32, (rows, 1), 0)
        first = history_start(bounds, row)

        def inner(p, total):
            col0 = pl.multiple_of(jnp.maximum(end - (p + 1) * wide, 0), rows)
            there = pl.ds(col0, wide)
            keys = act_ref[there, pl.ds(HEAD, HEAD)]
            values = act_ref[there, pl.ds(2 * HEAD, HEAD)]
            t = dot(query, keys, NT) * (0.5 * scale)
            col = col0 + lax.broadcasted_iota(jnp.int32, (1, wide), 1)
            last = jnp.minimum(row, end - p * wide - 1)
            mask = (col <= last) & (col >= first)
            weights = jnp.where(mask, t * (1.0 + jnp.tanh(t)), 0.0).astype(BF16)
            return total + dot(weights, values)

        count = (end - history_start(bounds, row0) + wide - 1) // wide
        att = lax.fori_loop(0, count, inner, jnp.zeros((rows, HEAD), F32)) * (1.0 / 1024)
        att_t = att.T
        att_ref[:, here] = att_t
        cot_t = cot_ref[here, :].astype(F32).T
        mean = jnp.mean(att_t, axis=0, keepdims=True)
        centred = att_t - mean
        stat_ref[:, here] = jnp.concatenate(
            [
                mean,
                jnp.sum(centred * centred, axis=0, keepdims=True),
                jnp.sum(cot_t * centred, axis=0, keepdims=True),
                jnp.sum(cot_t, axis=0, keepdims=True),
            ],
            axis=0,
        )
        return carry

    lax.fori_loop(0, act_ref.shape[0] // rows, block, 0)


def bwd_kernel(rows, scale, inv_root, bounds_ref, order_ref, act_ref, att_ref, cot_ref, stat0_ref,
               stat1_ref, stat2_ref, stat3_ref, normed_any, pre_any, mine_ref, theirs_ref, gw_ref,
               normed_s, pre_s, sems, keys_t, n_s, dq_s, dk_s, dv_s, both_s, gw_s):
    bounds = (bounds_ref[0], bounds_ref[1])
    wide = 2 * rows
    width = HEADS * HEAD
    total = act_ref.shape[0]
    fetches = (
        pltpu.make_async_copy(normed_any, normed_s, sems.at[0]),
        pltpu.make_async_copy(pre_any, pre_s, sems.at[1]),
    )
    for fetch in fetches:
        fetch.start()
    dk_s[...] = jnp.zeros_like(dk_s)
    dv_s[...] = jnp.zeros_like(dv_s)
    keys_t[...] = act_ref[:, pl.ds(HEAD, HEAD)].T

    def block(i, carry):
        row0 = pl.multiple_of(i * rows, rows)
        here = pl.ds(row0, rows)
        end = row0 + rows
        stats = [ref[:, here] for ref in (stat0_ref, stat1_ref, stat2_ref, stat3_ref)]
        means, second, cross, sums = (
            jnp.concatenate([s[r + k : r + k + 1] for s in stats for r in (0, 4)], axis=0)
            for k in range(4)
        )
        mean = jnp.mean(means, axis=0, keepdims=True)
        shift = means - mean
        var = jnp.sum(second + HEAD * shift * shift, axis=0, keepdims=True) * (1.0 / width)
        factor = lax.rsqrt(var + EPS)
        mean_cot = jnp.sum(sums, axis=0, keepdims=True) * (1.0 / width)
        inner_mean = factor * jnp.sum(cross + shift * sums, axis=0, keepdims=True) * (1.0 / width)
        n_t = (att_ref[:, here] - mean) * factor
        cot_t = cot_ref[here, :].astype(F32).T
        ga_t = factor * (cot_t - mean_cot - n_t * inner_mean)
        n_s[here, :] = n_t.T.astype(BF16)
        grad_att = ga_t.T.astype(BF16)
        query = act_ref[here, pl.ds(0, HEAD)]
        row = row0 + lax.broadcasted_iota(jnp.int32, (1, rows), 1)
        first = history_start(bounds, row)

        def inner(p, total_q):
            col0 = pl.multiple_of(jnp.maximum(end - (p + 1) * wide, 0), rows)
            there = pl.ds(col0, wide)
            keys = act_ref[there, pl.ds(HEAD, HEAD)]
            values = act_ref[there, pl.ds(2 * HEAD, HEAD)]
            t = dot(keys, query, NT) * (0.5 * scale)
            prod = dot(values, grad_att, NT)
            col = col0 + lax.broadcasted_iota(jnp.int32, (wide, 1), 0)
            last = jnp.minimum(row, end - p * wide - 1)
            mask = (col <= last) & (col >= first)
            th = jnp.tanh(t)
            up = 1.0 + th
            weights = jnp.where(mask, t * up, 0.0).astype(BF16)
            grads = jnp.where(mask, prod * (up * (1.0 + t * (1.0 - th))), 0.0).astype(BF16)
            dv_s[there, :] += dot(weights, grad_att)
            dk_s[there, :] += dot(grads, query)
            return total_q + dot(keys_t[:, there], grads)

        count = (end - history_start(bounds, row0) + wide - 1) // wide
        dq_s[here, :] = lax.fori_loop(0, count, inner, jnp.zeros((HEAD, rows), F32)).T
        return carry

    lax.fori_loop(0, total // rows, block, 0)
    for fetch in fetches:
        fetch.wait()

    def late(i, carry):
        here = pl.ds(pl.multiple_of(i * wide, wide), wide)
        inv = 1.0 / 1024
        gpre = jnp.concatenate(
            [
                dq_s[here, :] * (0.5 * inv * scale),
                dk_s[here, :] * (0.5 * inv * scale),
                dv_s[here, :] * inv,
            ],
            axis=1,
        )
        gpre = (gpre * silu_grad(pre_s[here, :])).astype(BF16)
        both_s[:, pl.ds(0, HEAD)] = n_s[here, :]
        both_s[:, pl.ds(HEAD, 3 * HEAD)] = gpre
        mine_ref[i] = both_s[pl.ds(pl.multiple_of((order_ref[0] % 2) * rows, rows), rows), :]
        theirs_ref[i] = both_s[pl.ds(pl.multiple_of((1 - order_ref[0] % 2) * rows, rows), rows), :]
        term = dot(gpre, normed_s[here, :], TN)

        @pl.when(i == 0)
        def _():
            gw_s[...] = term

        @pl.when(i > 0)
        def _():
            gw_s[...] += term

        return carry

    lax.fori_loop(0, total // wide, late, 0)
    gw_ref[...] = (gw_s[...].T * inv_root).astype(BF16)


def out_kernel(rows, heads_ref, got0_ref, got1_ref, got2_ref, got3_ref, w_ref, x_ref, cot_ref,
               out_ref, gtok_ref, g_s, acc_s):
    step = pl.program_id(0)
    width = HEADS * HEAD
    part = w_ref.shape[0]

    @pl.when(step == 0)
    def _():
        for s, got_ref in enumerate((got0_ref, got1_ref, got2_ref, got3_ref)):
            for j in range(2):
                col = pl.multiple_of(heads_ref[2 * s + j] * HEAD, HEAD)
                out_ref[:, pl.ds(col, HEAD)] = (
                    x_ref[:, pl.ds(col, HEAD)].astype(F32) + got_ref[j, :, pl.ds(0, HEAD)].astype(F32)
                ).astype(BF16)
                for t in range(3):
                    g_s[:, pl.ds(t * width + col, HEAD)] = got_ref[j, :, pl.ds((t + 1) * HEAD, HEAD)]

    acc_s[step] = dot(g_s[...], w_ref[...], NT)

    @pl.when(step == pl.num_programs(0) - 1)
    def _():
        x = x_ref[...].astype(F32)
        centred = x - jnp.mean(x, axis=-1, keepdims=True)
        factor = lax.rsqrt(jnp.mean(centred * centred, axis=-1, keepdims=True) + EPS)
        normal = centred * factor
        grad = jnp.concatenate([acc_s[i] for i in range(width // part)], axis=1)
        back = factor * (
            grad
            - jnp.mean(grad, axis=-1, keepdims=True)
            - normal * jnp.mean(grad * normal, axis=-1, keepdims=True)
        )
        gtok_ref[...] = (cot_ref[...].astype(F32) + back).astype(BF16)


def join_kernel(piece, where_ref, *refs):
    same, other = refs[:4], refs[4:8]
    out_ref, buf, sem = refs[8:]
    step = pl.program_id(0)

    def fetch(q, wait):
        for side, group in enumerate((same, other)):
            rel = lax.rem(q - where_ref[side] + 4, 4)
            slot = lax.rem(q, 2)
            for a, ref in enumerate(group):

                @pl.when(rel == a)
                def _():
                    copy = pltpu.make_async_copy(ref, buf.at[slot, side], sem.at[slot, side])
                    copy.wait() if wait else copy.start()

    @pl.when(step == 0)
    def _():
        fetch(step, False)

    @pl.when(step + 1 < pl.num_programs(0))
    def _():
        fetch(step + 1, False)

    fetch(step, True)
    slot = lax.rem(step, 2)
    for side in range(2):
        for s in range(4):
            head = where_ref[2 + 4 * side + s]
            for t in range(3):
                col = pl.multiple_of((t * HEADS + head) * HEAD, HEAD)
                out_ref[:, pl.ds(col, HEAD)] = buf[slot, side, s, :, pl.ds(t * HEAD, HEAD)].astype(F32)


def params(n):
    return pltpu.CompilerParams(dimension_semantics=("arbitrary",) * n, vmem_limit_bytes=VMEM)


IN_VMEM = pl.BlockSpec(memory_space=pltpu.VMEM)
IN_SMEM = pl.BlockSpec(memory_space=pltpu.SMEM)
ANYWHERE = pl.BlockSpec(memory_space=pl.ANY)


def shape(dims, dtype):
    return jax.ShapeDtypeStruct(dims, dtype)


SIDE = 4


def ring(axis, step):
    pairs = []
    for place in range(2 * SIDE**3):
        core = place % 2
        at = [place // (2 * SIDE * SIDE), place // (2 * SIDE) % SIDE, place // 2 % SIDE]
        at[axis(core)] = (at[axis(core)] + step) % SIDE
        pairs.append((place, ((at[0] * SIDE + at[1]) * SIDE + at[2]) * 2 + core))
    return pairs


def along(axis):
    return lambda value, step: lax.ppermute(value, ("dp", "ctx"), ring(axis, step))


def along_z(value, step):
    return lax.ppermute(value, "ctx", [(c, (c + 2 * step) % 8) for c in range(8)])


def swap(value):
    return lax.ppermute(value, "ctx", [(c, c ^ 1) for c in range(8)])


def pick(value, index):
    return lax.dynamic_index_in_dim(value, index, 0, keepdims=False)


def exchange(mine, theirs, z):
    theirs = swap(theirs)
    send = lambda d: jnp.stack([pick(mine, (z + d) % SIDE), pick(theirs, (z + d) % SIDE)])
    from_far, from_before, from_after = (along_z(send(d), d) for d in (2, 1, -1))
    return send(0), from_before, from_after, from_far


def body(tokens, cotangent, proj_weight, segment):
    x_tok = tokens[0]
    grad_out = cotangent[0]
    seg_ids = segment[0]
    rows, width = x_tok.shape
    ctx_count = lax.axis_size("ctx")
    dp_count = lax.axis_size("dp")
    total = rows * ctx_count
    scale = 1.0 / HEAD**0.5
    inv_root = 1.0 / (dp_count * total) ** 0.5
    head = lax.axis_index("ctx")
    core, z = head % 2, head // 2
    x_at, y_at = lax.axis_index("dp") // SIDE, lax.axis_index("dp") % SIDE
    chips_at = [z, (z + 3) % SIDE, (z + 1) % SIDE, (z + 2) % SIDE]
    order = jnp.stack([2 * p + c for p in chips_at for c in (core, 1 - core)]).astype(jnp.int32)

    before = along_z(x_tok, 1)
    after = along_z(x_tok, -1)
    w_head = jnp.concatenate(
        [lax.dynamic_slice_in_dim(proj_weight, t * width + head * HEAD, HEAD, 1) for t in range(3)],
        axis=1,
    )

    def project(chip, starts, shards, earlier):
        return pl.pallas_call(
            lambda *refs: proj_kernel(rows, starts, *refs),
            grid_spec=pltpu.PrefetchScalarGridSpec(
                num_scalar_prefetch=1,
                grid=(1,),
                in_specs=[pl.BlockSpec(v.shape, lambda i, o: (0, 0)) for v in shards]
                + [pl.BlockSpec((width, 3 * HEAD), lambda i, o: (0, 0))]
                + [ANYWHERE] * len(earlier),
                out_specs=[
                    pl.BlockSpec((2 * rows, width), lambda i, o: (o[0], 0)),
                    pl.BlockSpec((2 * rows, 3 * HEAD), lambda i, o: (o[0], 0)),
                    pl.BlockSpec((2 * rows, 3 * HEAD), lambda i, o: (o[0], 0)),
                    pl.BlockSpec((8, HEAD), lambda i, o: (0, 0)),
                ],
            ),
            out_shape=[
                shape((total, width), BF16),
                shape((total, 3 * HEAD), F32),
                shape((total, 3 * HEAD), BF16),
                shape((8, HEAD), F32),
            ],
            input_output_aliases={2 + len(shards) + i: i for i in range(len(earlier))},
            compiler_params=params(1),
            cost_estimate=pl.CostEstimate(flops=1, bytes_accessed=1, transcendentals=0),
            name="project",
        )(jnp.stack([chip, core]).astype(jnp.int32), *shards, w_head, *earlier)

    after_token = lambda value, token: value + token[0, 0].astype(value.dtype)
    whole = ((0, 0), (1, 0))
    half = rows // 2
    *seen, token = project(z, whole, (x_tok, swap(x_tok)), ())
    far_low = along_z(after_token(before[:half], token), 1)
    far_high = along_z(after_token(after[half:], token), -1)

    counts = jnp.stack([jnp.sum(seg_ids < 1), jnp.sum(seg_ids < 2)]).astype(BF16)
    cot_chunks = jnp.concatenate(
        [
            grad_out.reshape(rows, HEADS, HEAD).transpose(1, 0, 2),
            jnp.broadcast_to(jnp.pad(counts, (0, HEAD - 2))[None, None], (HEADS, 16, HEAD)),
        ],
        axis=1,
    ).reshape(SIDE, 2, rows + 16, HEAD)
    cot_got = exchange(
        lax.dynamic_index_in_dim(cot_chunks, core, 1, keepdims=False),
        lax.dynamic_index_in_dim(cot_chunks, 1 - core, 1, keepdims=False),
        z,
    )
    bounds = sum(jnp.sum(v[:, rows, :2].astype(F32), axis=0) for v in cot_got).astype(jnp.int32)

    *seen, token = project(chips_at[1], whole, (before, swap(before)), seen)
    *seen, token = project(chips_at[2], whole, (after, swap(after)), seen)
    halves = ((0, 0), (0, half), (1, 0), (1, half))
    far = (far_low, far_high, swap(after_token(far_low, token)), swap(after_token(far_high, token)))
    normed, pre, act, token = project(chips_at[3], halves, far, seen)

    att_t, stat, cot_head = pl.pallas_call(
        lambda *refs: fwd_kernel(rows, scale, *refs),
        in_specs=[IN_SMEM, IN_SMEM] + [IN_VMEM] * 5,
        out_specs=[IN_VMEM] * 3,
        out_shape=[shape((HEAD, total), F32), shape((4, total), F32), shape((total, HEAD), BF16)],
        compiler_params=params(0),
        name="attend",
    )(order, bounds, act, *cot_got)

    pair = jnp.concatenate([stat, swap(stat)], axis=0)
    stats = (pair, along_z(pair, 2), along_z(pair, 1), along_z(pair, -1))

    mine, theirs, gw = pl.pallas_call(
        lambda *refs: bwd_kernel(rows, scale, inv_root, *refs),
        in_specs=[IN_SMEM, IN_SMEM] + [IN_VMEM] * 7 + [ANYWHERE] * 2,
        out_specs=[IN_VMEM] * 3,
        out_shape=[
            shape((SIDE, rows, 4 * HEAD), BF16),
            shape((SIDE, rows, 4 * HEAD), BF16),
            shape((width, 3 * HEAD), BF16),
        ],
        scratch_shapes=[
            pltpu.VMEM((total, width), BF16),
            pltpu.VMEM((total, 3 * HEAD), F32),
            pltpu.SemaphoreType.DMA((2,)),
            pltpu.VMEM((HEAD, total), BF16),
            pltpu.VMEM((total, HEAD), BF16),
            pltpu.VMEM((total, HEAD), F32),
            pltpu.VMEM((total, HEAD), F32),
            pltpu.VMEM((total, HEAD), F32),
            pltpu.VMEM((2 * rows, 4 * HEAD), BF16),
            pltpu.VMEM((3 * HEAD, width), F32),
        ],
        compiler_params=params(0),
        name="attend_back",
    )(bounds, order, act, att_t, cot_head, *stats, normed, pre)

    first_way = along(lambda c: c)
    other_way = along(lambda c: 1 - c)
    piece = width // SIDE
    my_piece = jnp.where(core == 0, x_at, y_at)
    cut = lambda d: lax.dynamic_slice_in_dim(gw, (my_piece + d) % SIDE * piece, piece, 0)
    up = lambda v: v.astype(F32)
    terms = [first_way(cut(d), d) for d in (2, 1, -1)]
    summed = ((up(cut(0)) + up(terms[0])) + (up(terms[1]) + up(terms[2]))).astype(BF16)
    terms = [other_way(summed, d) for d in (2, 1, -1)]
    summed = ((up(summed) + up(terms[0])) + (up(terms[1]) + up(terms[2]))).astype(BF16)
    got = exchange(mine, theirs, z)
    summed = summed + (0.0 * jnp.abs(got[3][0, 0, 0]).astype(F32)).astype(BF16)
    chips = jnp.stack([summed, along_z(summed, 1), along_z(summed, -1), along_z(summed, 2)])
    same = [chips, first_way(chips, -1), first_way(chips, 2), first_way(chips, 1)]
    other = [swap(v) for v in same]
    z_order = jnp.stack([z, (z + 3) % SIDE, (z + 1) % SIDE, (z + 2) % SIDE])
    where = jnp.concatenate(
        [
            jnp.stack([my_piece, jnp.where(core == 0, y_at, x_at)]),
            2 * z_order + core,
            2 * z_order + 1 - core,
        ]
    ).astype(jnp.int32)
    grad_weight = pl.pallas_call(
        lambda *refs: join_kernel(piece, *refs),
        grid_spec=pltpu.PrefetchScalarGridSpec(
            num_scalar_prefetch=1,
            grid=(SIDE,),
            in_specs=[pl.BlockSpec(memory_space=pl.ANY)] * 8,
            out_specs=pl.BlockSpec((piece, 3 * width), lambda i, w: (i, 0)),
            scratch_shapes=[
                pltpu.VMEM((2, 2, SIDE, piece, 3 * HEAD), BF16),
                pltpu.SemaphoreType.DMA((2, 2)),
            ],
        ),
        out_shape=jax.ShapeDtypeStruct((width, 3 * width), F32),
        compiler_params=params(1),
        name="join",
    )(where, *same, *other)

    part = 512
    output, grad_tok = pl.pallas_call(
        lambda *refs: out_kernel(rows, *refs),
        grid_spec=pltpu.PrefetchScalarGridSpec(
            num_scalar_prefetch=1,
            grid=(width // part,),
            in_specs=[pl.BlockSpec((2, rows, 4 * HEAD), lambda i, o: (0, 0, 0))] * 4
            + [
                pl.BlockSpec((part, 3 * width), lambda i, o: (i, 0)),
                pl.BlockSpec((rows, width), lambda i, o: (0, 0)),
                pl.BlockSpec((rows, width), lambda i, o: (0, 0)),
            ],
            out_specs=[
                pl.BlockSpec((rows, width), lambda i, o: (0, 0)),
                pl.BlockSpec((rows, width), lambda i, o: (0, 0)),
            ],
            scratch_shapes=[
                pltpu.VMEM((rows, 3 * width), BF16),
                pltpu.VMEM((width // part, rows, part), F32),
            ],
        ),
        out_shape=[jax.ShapeDtypeStruct((rows, width), BF16)] * 2,
        compiler_params=params(1),
        cost_estimate=pl.CostEstimate(flops=1, bytes_accessed=1, transcendentals=0),
        name="finish",
    )(order, *got, proj_weight, x_tok, grad_out)
    return (output[None], grad_tok[None], grad_weight)


def solution(mesh):
    in_specs = (P("dp", "ctx", None), P("dp", "ctx", None), P(), P("dp", "ctx"))
    out_specs = (P("dp", "ctx", None), P("dp", "ctx", None), P())
    return jax.shard_map(body, mesh=mesh, in_specs=in_specs, out_specs=out_specs, check_vma=False)
```
